256 devices in a mesh: lat: 32 (over x, y, core), lev: 8 (over z).
Axes of the slice: x: 4, y: 4, z: 8, core: 2. Of those that a mesh axis runs over, the one named last changes fastest.
Arguments:
- grid_field: bfloat16 [1280, 64, 2560], P('lat', 'lev'), may hold values from -6 to 6
- lon_count: int32 [1280], P('lat'), may hold values from 20 to 2560, as said below
- wave_table: int32 [1280], replicated, may hold values from 0 to 1279, as said below
- legendre: bfloat16 [1280, 640, 1280], P(('lat', 'lev')), may hold values from -0.25 to 0.25
- vertical: float32 [64, 64], replicated, may hold values from -0.8 to 2.5, as said below
Outputs:
- spectral: float32 [64, 2, 1280, 1280], P(None, None, ('lat', 'lev'))
The draws below stay inside these ranges and needn't reach their ends.
Inputs may be any that keep to these rules, and one draw needn't show every extreme that they name: `lon_count`: multiples of 4, 2560 at the two latitudes next to the equator, 20 at the poles. `wave_table`: A permutation of the wavenumbers: slot r of group g holds r * 256 + p(g) for even r and r * 256 + 255 - p(g) for odd r, for one permutation p of the groups. `vertical`: zero where the two level indices differ by more than 2; diagonal entries 1 or more.
All inputs are finite; a program needn't handle non-finite values.
Results may differ from the reference program's by a relative error of at most 0.0049.
Values may be sent and summed in bfloat16 or wider, within the bound.
A program may use at most 64 MiB of HBM per device.

```python
import math
import jax
import jax.numpy as jnp
from jax import lax

NLON = 2560
NLAT = 1280
NT = 1280
NLEV = 64
GROUPS = 256
MDEV = 5


def draw_lon_count(key, part):
    key = jax.random.fold_in(key, 11)
    latitude = jnp.arange(NLAT, dtype=jnp.int32)
    distance = jnp.minimum(latitude, NLAT - 1 - latitude)
    baseline = 20 + (NLON - 20) * (distance + 1) // (NLAT // 2)
    baseline = baseline // 4 * 4
    jitter = 4 * jax.random.randint(key, (NLAT,), 0, 9)
    jitter = jnp.where(distance == NLAT // 2 - 1, 0, jitter)
    return jnp.clip(baseline - jitter, 20, NLON).astype(jnp.int32)


def draw_wave_table(key, part):
    key = jax.random.fold_in(key, 23)
    shuffle = jax.random.permutation(key, GROUPS).astype(jnp.int32)
    slot_index = jnp.arange(NT, dtype=jnp.int32)
    group_index = slot_index // MDEV
    round_index = slot_index % MDEV
    group_rank = shuffle[group_index]
    position = jnp.where(round_index % 2 == 0, group_rank, GROUPS - 1 - group_rank)
    return (round_index * GROUPS + position).astype(jnp.int32)


def draw_vertical(key, part):
    key = jax.random.fold_in(key, 37)
    key_off, key_diag = jax.random.split(key)
    row_index = jnp.arange(NLEV, dtype=jnp.int32)[:, None]
    col_index = jnp.arange(NLEV, dtype=jnp.int32)[None, :]
    distance = jnp.abs(row_index - col_index)
    off_band = jnp.clip(jax.random.normal(key_off, (NLEV, NLEV), jnp.float32) * 0.35, -0.8, 0.8)
    diagonal = jax.random.uniform(key_diag, (NLEV, NLEV), jnp.float32, 1.0, 2.0)
    return jnp.where(distance == 0, diagonal, jnp.where(distance <= 2, off_band, 0.0)).astype(jnp.float32)


def levels(key, dims, cuts, smallest, largest):
    level = 1.0
    for axis_at, blocks in cuts:
        steps = jax.random.uniform(jax.random.fold_in(jax.random.fold_in(key, 6), axis_at), (blocks,), jnp.float32, smallest / len(cuts), largest / len(cuts))
        level = level * jnp.repeat(jnp.exp(steps), dims[axis_at] // blocks).reshape((-1,) + (1,) * (len(dims) - 1 - axis_at))
    return level


def gaussian(own_key, dims, scale, reach, shards=(), kind=jnp.bfloat16):
    array = scale * jax.random.normal(own_key, dims, jnp.float32)
    if shards:
        array = array * levels(own_key, dims, shards, -0.22, 0.18)
    return jnp.clip(array, -reach, reach).astype(kind)


def setup_inputs(seed: int = 0) -> dict:
    streams_of = jax.random.split(jax.random.key(seed), 6)
    return {
        "grid_field": gaussian(streams_of[0], (NLAT, NLEV, NLON), 1.0, 6.0, ((0, 32), (1, 8))),
        "lon_count": draw_lon_count(jax.random.fold_in(streams_of[5], 71), 0),
        "wave_table": draw_wave_table(jax.random.fold_in(streams_of[5], 71), 0),
        "legendre": gaussian(streams_of[3], (NT, NLAT // 2, NT), (NLAT // 2) ** -0.5, 0.25, ((0, 256),)),
        "vertical": draw_vertical(jax.random.fold_in(streams_of[5], 71), 0),
    }


def fourier_basis(waves, length):
    points = lax.broadcasted_iota(jnp.int32, (length, waves.shape[0]), 0)
    phases = points * waves[None, :].astype(jnp.int32) % length
    angles = phases.astype(jnp.float32) * jnp.float32(2.0 * math.pi / length)
    factor = jnp.float32(math.sqrt(2.0 / length))
    return jnp.concatenate([jnp.cos(angles) * factor, -jnp.sin(angles) * factor], axis=1).astype(jnp.bfloat16)

def legendre_block(blocks):
    table, symmetric, antisym = blocks
    half_waves = table.shape[2] // 2
    table = table.astype(jnp.float32)
    even_part = jnp.einsum('slq,slvc->svcq', table[:, :, :half_waves], symmetric.astype(jnp.float32), precision=lax.Precision.HIGHEST)
    odd_part = jnp.einsum('slq,slvc->svcq', table[:, :, half_waves:], antisym.astype(jnp.float32), precision=lax.Precision.HIGHEST)
    return jnp.concatenate([even_part, odd_part], axis=3)

def reference(grid_field, lon_count, wave_table, legendre, vertical):
    lat_count, lev_count, lon_points = grid_field.shape
    wave_count = wave_table.shape[0]
    basis = fourier_basis(wave_table, lon_points)
    fourier = jnp.dot(grid_field.reshape(lat_count * lev_count, lon_points), basis, preferred_element_type=jnp.float32)
    fourier = fourier.reshape(lat_count, lev_count, 2, wave_count)
    retained = 2 * wave_table[None, :] < lon_count[:, None]
    fourier = jnp.where(retained[:, None, None, :], fourier, jnp.zeros_like(fourier)).astype(jnp.bfloat16)
    half_lat = lat_count // 2
    northern = fourier[:half_lat].astype(jnp.float32)
    southern = fourier[half_lat:][::-1].astype(jnp.float32)
    symmetric = jnp.moveaxis((northern + southern).astype(jnp.bfloat16), 3, 0)
    antisym = jnp.moveaxis((northern - southern).astype(jnp.bfloat16), 3, 0)
    block_size = math.gcd(wave_count, 16)
    shaped = (wave_count // block_size, block_size)
    projected = lax.map(legendre_block, (legendre.reshape(shaped + legendre.shape[1:]), symmetric.reshape(shaped + symmetric.shape[1:]), antisym.reshape(shaped + antisym.shape[1:])))
    projected = jnp.moveaxis(projected.reshape((wave_count,) + projected.shape[2:]), 0, 2)
    half_waves = wave_count // 2
    degree = jnp.arange(wave_count, dtype=jnp.int32)
    offset = jnp.where(degree < half_waves, 2 * degree, 2 * (degree - half_waves) + 1)
    in_range = wave_table[:, None] + offset[None, :] < wave_count
    projected = jnp.where(in_range[None, None], projected, jnp.zeros_like(projected))
    return jnp.einsum('wv,wcsq->vcsq', vertical, projected, precision=lax.Precision.HIGHEST)
```

```python
import functools
import math

import jax
import jax.numpy as jnp
import ml_dtypes
import numpy as np
from jax import lax
from jax.experimental import pallas as pl
from jax.experimental.pallas import tpu as pltpu
from jax.sharding import PartitionSpec as P

MESH = pl.DeviceIdType.MESH
NLON = 2560
NT = 1280
HALF = 640
ROUNDS = 5
WAVES = 256
LATS = 32
LEVS = 8
ROWS = 40
PAD = 48
NV = 8
F32 = jnp.float32
BF16 = jnp.bfloat16


def basis_constant():
    points = np.arange(NLON, dtype=np.int64)
    column = np.arange(WAVES, dtype=np.int64)
    factor = np.float32(math.sqrt(2.0 / NLON))
    rounds = []
    for r in range(ROUNDS):
        waves = r * WAVES + (column if r % 2 == 0 else WAVES - 1 - column)
        phases = points[:, None] * waves[None, :] % NLON
        angles = phases.astype(np.float32) * np.float32(2.0 * math.pi / NLON)
        rounds.append(np.concatenate([np.cos(angles) * factor, -np.sin(angles) * factor], axis=1))
    return np.stack(rounds).astype(ml_dtypes.bfloat16)


def iota(shape, dim):
    return lax.broadcasted_iota(jnp.int32, shape, dim)


def one_hot(mask):
    return jnp.where(mask, 1.0, 0.0).astype(BF16)


def dot(a, b):
    return jnp.dot(a, b, preferred_element_type=F32)


def dot_nt(a, b):
    return lax.dot_general(a, b, (((1,), (1,)), ((), ())), preferred_element_type=F32)


def kernel(
    wave_ref, lon_ref, target_ref, vertical_ref, grid_ref, basis_ref, legendre_ref,
    out_ref,
    x, basis, table, lon, route, order, mix, folded, sent, got, turned, ready, result,
    in_sem, basis_sem, table_sem, out_sem, lat_send, lat_recv, lev_send, lev_recv,
):
    me = lax.axis_index("lat")
    lev = lax.axis_index("lev")

    grid_copy = pltpu.make_async_copy(grid_ref, x, in_sem)
    grid_copy.start()
    basis_copies = [pltpu.make_async_copy(basis_ref.at[r], basis.at[r], basis_sem.at[r]) for r in range(ROUNDS)]
    for copy in basis_copies:
        copy.start()
    table_copies = []
    for r in range(ROUNDS):
        width = HALF - 128 * r
        for part in range(2):
            block = (r, slice(None), pl.ds(part * HALF, width))
            table_copies.append(
                pltpu.make_async_copy(legendre_ref.at[block], table.at[block], table_sem.at[r, part])
            )
    for copy in table_copies:
        copy.start()

    barrier = pltpu.get_barrier_semaphore()

    def greet_lat(k, carry):
        pl.semaphore_signal(barrier, inc=1, device_id=(lax.rem(me + k, LATS), lev), device_id_type=MESH)
        return carry

    def greet_lev(k, carry):
        pl.semaphore_signal(barrier, inc=1, device_id=(me, lax.rem(lev + k, LEVS)), device_id_type=MESH)
        return carry

    lax.fori_loop(1, LATS, greet_lat, 0)
    lax.fori_loop(1, LEVS, greet_lev, 0)

    for t in range(ROWS):
        lon[pl.ds(t * NV, NV), :] = jnp.full((NV, 128), lon_ref[t], jnp.int32)
    route[...] = one_hot(iota((2 * WAVES, 2 * WAVES), 0) == target_ref[...])
    row = iota((NV * PAD, ROWS * NV), 0)
    col = iota((NV * PAD, ROWS * NV), 1)
    at = lax.rem(row, PAD)
    at = jnp.where(me < LATS // 2, at, ROWS - 1 - at)
    order[...] = one_hot((lax.div(col, NV) == at) & (lax.rem(col, NV) == lax.div(row, PAD)))

    lane_block = lax.div(iota((PAD, 128), 1), 16)

    def send_lat(r):
        def start(k, carry):
            peer = lax.rem(me + k, LATS)
            pltpu.make_async_remote_copy(
                src_ref=sent.at[r, peer],
                dst_ref=got.at[r, me],
                send_sem=lat_send.at[r],
                recv_sem=lat_recv.at[r],
                device_id=(peer, lev),
                device_id_type=MESH,
            ).start()
            return carry

        lax.fori_loop(1, LATS, start, 0)

    def fourier(r):
        values = dot(x[...].reshape(ROWS * NV, NLON), basis[r])
        column = iota((8, 2 * WAVES), 1) & (WAVES - 1)
        odd = lax.rem(r, 2) == 1
        waves = r * WAVES + jnp.where(odd, WAVES - 1 - column, column)
        twice = jnp.broadcast_to(2 * waves[:1], (ROWS * NV, 2 * WAVES))
        longitudes = jnp.concatenate([lon[...]] * 4, axis=1)
        values = jnp.where(twice < longitudes, values, 0.0).astype(BF16)
        values = dot(order[...], values).astype(BF16)
        values = dot(values, route[...])
        for high in range(LATS // 8):
            blocks = []
            for v in range(NV):
                block = values[v * PAD : (v + 1) * PAD, high * 128 : (high + 1) * 128]
                blocks.append(pltpu.roll(block, 16 * v, 1) if v else block)
            for bit in range(3):
                taken = (lane_block >> bit) & 1 == 1
                blocks = [jnp.where(taken, blocks[(i + (1 << bit)) % 8], blocks[i]) for i in range(8)]
            for low in range(8):
                sent[r, high * 8 + low] = blocks[-low % 8].astype(BF16)

    def turn(r):
        pltpu.make_async_copy(got.at[r, pl.ds(0, LATS - 1)], got.at[r, pl.ds(0, LATS - 1)], lat_recv.at[r]).wait()
        got[r, me] = sent[r, me]
        for i in range(LATS // 2):
            north = got[r, i].astype(F32)[:ROWS]
            south = got[r, LATS - 1 - i].astype(F32)[:ROWS]
            folded[0, pl.ds(i * ROWS, ROWS), :] = north + south
            folded[1, pl.ds(i * ROWS, ROWS), :] = north - south
        row = iota((128, 128), 0)
        col = iota((128, 128), 1)
        level = row & 7
        source = 16 * ((level + me) & 7) + 8 * ((row >> 3) & 1) + (row >> 4)
        pick = one_hot(col == source)
        for part in range(2):
            values = dot_nt(pick, folded[part].astype(BF16)).astype(BF16)
            turned[r, :, :, pl.ds(part * HALF, HALF)] = values.reshape(LEVS, 16, HALF)

        def start(k, carry):
            peer = lax.rem(lev + k, LEVS)
            pltpu.make_async_remote_copy(
                src_ref=turned.at[r, peer],
                dst_ref=ready.at[r, lev],
                send_sem=lev_send.at[r],
                recv_sem=lev_recv.at[r],
                device_id=(me, peer),
                device_id_type=MESH,
            ).start()
            return carry

        lax.fori_loop(1, LEVS, start, 0)

    def vertical_operator():
        row = iota((128, 64), 0)
        pick_out = one_hot(iota((128, 64), 1) == (row >> 1))
        col = iota((64, 128), 1)
        pick_in = one_hot(iota((64, 128), 0) == 8 * (col >> 4) + (col & 7))
        same = (iota((128, 128), 0) & 1) == ((iota((128, 128), 1) >> 3) & 1)
        whole = vertical_ref[...]
        high = whole.astype(BF16)
        low = (whole - high.astype(F32)).astype(BF16)
        for k, term in enumerate((high, low)):
            term = dot_nt(pick_out, term).astype(BF16)
            term = dot(term, pick_in)
            mix[:, pl.ds(128 * k, 128)] = jnp.where(same, term, 0.0).astype(BF16)

    def legendre(r):
        pltpu.make_async_copy(ready.at[r, pl.ds(0, LEVS - 1)], ready.at[r, pl.ds(0, LEVS - 1)], lev_recv.at[r]).wait()
        ready[r, lev] = turned[r, lev]
        width = HALF - 128 * r
        wave = wave_ref[(me * LEVS + lev) * ROUNDS + r]
        table_copies[2 * r].wait()
        table_copies[2 * r + 1].wait()
        values = ready[r].reshape(128, NT)
        mixed = dot(mix[...], jnp.concatenate([values, values], axis=0)).astype(BF16)
        for part in range(2):
            total = dot(mixed[:, part * HALF : (part + 1) * HALF], table[r, :, pl.ds(part * HALF, width)])
            degree = wave + 2 * iota((128, width), 1) + part
            result[r, :, pl.ds(part * HALF, width)] = jnp.where(degree < NT, total, 0.0)
            if width < HALF:
                result[r, :, pl.ds(part * HALF + width, HALF - width)] = jnp.zeros((128, HALF - width), F32)
        pltpu.make_async_copy(result.at[r], out_ref.at[r], out_sem.at[r]).start()

    grid_copy.wait()
    basis_copies[0].wait()
    fourier(0)
    pl.semaphore_wait(barrier, LATS - 1 + LEVS - 1)
    send_lat(0)
    vertical_operator()

    def step(r, carry):
        pltpu.make_async_copy(basis_ref.at[r], basis.at[r], basis_sem.at[r]).wait()
        fourier(r)
        send_lat(r)
        turn(r - 1)
        return carry

    lax.fori_loop(1, ROUNDS, step, 0)
    legendre(0)
    turn(ROUNDS - 1)
    for r in range(1, ROUNDS):
        legendre(r)
    for r in range(ROUNDS):
        pltpu.make_async_copy(result.at[r], out_ref.at[r], out_sem.at[r]).wait()
        pltpu.make_async_copy(sent.at[r, pl.ds(0, LATS - 1)], sent.at[r, pl.ds(0, LATS - 1)], lat_send.at[r]).wait()
        pltpu.make_async_copy(turned.at[r, pl.ds(0, LEVS - 1)], turned.at[r, pl.ds(0, LEVS - 1)], lev_send.at[r]).wait()


def on_device(grid_field, lon_count, wave_table, legendre, vertical):
    place = wave_table[::ROUNDS].reshape(LATS, 1, LEVS)
    target = place + WAVES * jnp.arange(2, dtype=jnp.int32)[None, :, None]
    anywhere = pl.BlockSpec(memory_space=pl.ANY)
    vmem = pl.BlockSpec(memory_space=pltpu.VMEM)
    smem = pl.BlockSpec(memory_space=pltpu.SMEM)
    result = pl.pallas_call(
        kernel,
        out_shape=jax.ShapeDtypeStruct((ROUNDS, 128, NT), F32),
        in_specs=[smem, smem, vmem, vmem, anywhere, anywhere, anywhere],
        out_specs=anywhere,
        scratch_shapes=[
            pltpu.VMEM((ROWS, NV, NLON), BF16),
            pltpu.VMEM((ROUNDS, NLON, 2 * WAVES), BF16),
            pltpu.VMEM((ROUNDS, HALF, NT), BF16),
            pltpu.VMEM((ROWS * NV, 128), jnp.int32),
            pltpu.VMEM((2 * WAVES, 2 * WAVES), BF16),
            pltpu.VMEM((NV * PAD, ROWS * NV), BF16),
            pltpu.VMEM((128, 256), BF16),
            pltpu.VMEM((2, HALF, 128), F32),
            pltpu.VMEM((ROUNDS, LATS, PAD, 128), BF16),
            pltpu.VMEM((ROUNDS, LATS, PAD, 128), BF16),
            pltpu.VMEM((ROUNDS, LEVS, 16, NT), BF16),
            pltpu.VMEM((ROUNDS, LEVS, 16, NT), BF16),
            pltpu.VMEM((ROUNDS, 128, NT), F32),
            pltpu.SemaphoreType.DMA,
            pltpu.SemaphoreType.DMA((ROUNDS,)),
            pltpu.SemaphoreType.DMA((ROUNDS, 2)),
            pltpu.SemaphoreType.DMA((ROUNDS,)),
            pltpu.SemaphoreType.DMA((ROUNDS,)),
            pltpu.SemaphoreType.DMA((ROUNDS,)),
            pltpu.SemaphoreType.DMA((ROUNDS,)),
            pltpu.SemaphoreType.DMA((ROUNDS,)),
        ],
        compiler_params=pltpu.CompilerParams(collective_id=0, has_side_effects=True, vmem_limit_bytes=56 << 20),
        cost_estimate=pl.CostEstimate(flops=6_000_000_000, bytes_accessed=24_000_000, transcendentals=0),
    )(wave_table, lon_count, target.reshape(1, 2 * WAVES), vertical, grid_field, jnp.asarray(basis_constant()), legendre)
    return result.reshape(ROUNDS, 64, 2, NT).transpose(1, 2, 0, 3)


def solution(mesh):
    return jax.shard_map(
        on_device,
        mesh=mesh,
        in_specs=(P("lat", "lev", None), P("lat"), P(), P(("lat", "lev"), None, None), P()),
        out_specs=P(None, None, ("lat", "lev"), None),
        check_vma=False,
    )
```

```python
import functools
import math

import jax
import jax.numpy as jnp
import ml_dtypes
import numpy as np
from jax import lax
from jax.experimental import pallas as pl
from jax.experimental.pallas import tpu as pltpu
from jax.sharding import PartitionSpec as P

MESH = pl.DeviceIdType.MESH
NLON = 2560
NT = 1280
HALF = 640
ROUNDS = 5
WAVES = 256
LATS = 32
LEVS = 8
ROWS = 40
PAD = 48
NV = 8
EDGE = 16
POLAR = 7
F32 = jnp.float32
BF16 = jnp.bfloat16


class Plan:
    def __init__(self, sparse):
        self.sparse = sparse
        if sparse:
            self.first_pair = [0] + [(128 * r - EDGE) // ROWS for r in range(1, ROUNDS)]
            self.chunks = [(0, 0, 256), (4, 512, HALF), (3, 384, HALF), (2, 256, HALF), (1, 128, HALF), (0, 256, HALF)]
            self.turn_step = [1, 1, 2, 3, 4, 5]
        else:
            self.first_pair = [0] * ROUNDS
            self.chunks = [(r, 0, HALF) for r in range(ROUNDS)]
            self.turn_step = [r + 1 for r in range(ROUNDS)]

    def pairs(self, chunk):
        r, low, high = self.chunks[chunk]
        edge = EDGE if self.sparse and r else 0
        return range((low - edge) // ROWS, -(-high // ROWS))

    def sources(self, chunk):
        r = self.chunks[chunk][0]
        if self.sparse and r == 0:
            return (0, POLAR) if chunk == 0 else (POLAR, LATS // 2)
        return (self.first_pair[r], LATS // 2)

    def table_start(self, r):
        return 128 * max(r - 1, 0) if self.sparse else 0


def basis_constant():
    points = np.arange(NLON // 2, dtype=np.int64)
    column = np.arange(WAVES, dtype=np.int64)
    factor = np.float32(math.sqrt(2.0 / NLON))
    rounds = []
    for r in range(ROUNDS):
        waves = r * WAVES + (column if r % 2 == 0 else WAVES - 1 - column)
        phases = points[:, None] * waves[None, :] % NLON
        angles = phases.astype(np.float32) * np.float32(2.0 * math.pi / NLON)
        cosines, sines = np.cos(angles) * factor, -np.sin(angles) * factor
        rounds.append(np.concatenate([cosines[:, 0::2], sines[:, 0::2], cosines[:, 1::2], sines[:, 1::2]], axis=1))
    return np.stack(rounds).astype(ml_dtypes.bfloat16)


def iota(shape, dim):
    return lax.broadcasted_iota(jnp.int32, shape, dim)


def one_hot(mask):
    return jnp.where(mask, 1.0, 0.0).astype(BF16)


def dot(a, b):
    return jnp.dot(a, b, preferred_element_type=F32)


def dot_nt(a, b):
    return lax.dot_general(a, b, (((1,), (1,)), ((), ())), preferred_element_type=F32)


def await_bytes(ref, semaphore):
    pltpu.make_async_copy(ref, ref, semaphore).wait()


def kernel(plan, *refs):
    (
        wave_ref, lon_ref, wave_row_ref, vertical_ref, grid_ref, basis_ref, legendre_ref,
        out_ref, flag_ref,
        x, basis, table, lon, route, order, mix, folded, edges, sent, got, edge_sent, edge_got, result, *chunk_refs,
    ) = refs
    count = len(plan.chunks)
    turned, ready = chunk_refs[:count], chunk_refs[count : 2 * count]
    (
        in_sem, basis_sem, table_sem, out_sem, lat_send, lat_recv, lev_send, lev_recv, edge_send, edge_recv,
    ) = chunk_refs[2 * count :]
    me = lax.axis_index("lat")
    lev = lax.axis_index("lev")
    pair = jnp.minimum(me, LATS - 1 - me)

    def sends(r):
        first = 0
        for k in range(1, ROUNDS):
            first = jnp.where(r == k, plan.first_pair[k], first)
        return pair >= first

    def round_at(step):
        if not plan.sparse:
            return step, step < ROUNDS
        usual = ROUNDS - 1 - step
        early = (pair < POLAR) & (step == 0)
        r = jnp.where(early, 0, usual)
        due = early | ((step > 0) | (pair >= POLAR)) & sends(usual) & ~((pair < POLAR) & (usual == 0))
        return jnp.maximum(r, 0), due & (usual >= 0)

    def basis_copy(r):
        return pltpu.make_async_copy(basis_ref.at[r], basis.at[r], basis_sem.at[r])

    grid_copy = pltpu.make_async_copy(grid_ref, x, in_sem)
    grid_copy.start()

    def start_basis(step, carry):
        r, due = round_at(step)

        @pl.when(due)
        def _():
            basis_copy(r).start()

        return carry

    lax.fori_loop(0, ROUNDS, start_basis, 0)
    table_copies = {}
    for r in reversed(range(ROUNDS)):
        start, width = plan.table_start(r), HALF - 128 * r
        for part in range(2):
            block = (r, pl.ds(start, HALF - start), pl.ds(part * HALF, width))
            copy = pltpu.make_async_copy(legendre_ref.at[block], table.at[block], table_sem.at[r, part])
            copy.start()
            table_copies[r, part] = copy

    barrier = pltpu.get_barrier_semaphore()

    def greet_lat(k, carry):
        pl.semaphore_signal(barrier, inc=1, device_id=(lax.rem(me + k, LATS), lev), device_id_type=MESH)
        return carry

    def greet_lev(k, carry):
        pl.semaphore_signal(barrier, inc=1, device_id=(me, lax.rem(lev + k, LEVS)), device_id_type=MESH)
        return carry

    lax.fori_loop(1, LATS, greet_lat, 0)
    lax.fori_loop(1, LEVS, greet_lev, 0)

    for t in range(ROWS):
        lon[pl.ds(t * NV, NV), :] = jnp.full((NV, 128), lon_ref[t], jnp.int32)
    row = iota((NT, 2 * WAVES), 0)
    col = iota((NT, 2 * WAVES), 1)
    pick = one_hot(row == ROUNDS * (8 * (col >> 4) + (col & 7)))
    waves = jnp.broadcast_to(wave_row_ref[...].astype(F32), (8, NT)).astype(BF16)
    place = dot(waves, pick).astype(jnp.int32)
    target = WAVES * (place & 1) + 128 * ((iota((8, 2 * WAVES), 1) >> 3) & 1) + (place >> 1)
    route[...] = one_hot(iota((2 * WAVES, 2 * WAVES), 0) == target[:1])
    row = iota((NV * PAD, ROWS * NV), 0)
    col = iota((NV * PAD, ROWS * NV), 1)
    at = lax.rem(row, PAD)
    at = jnp.where(me < LATS // 2, at, ROWS - 1 - at)
    order[...] = one_hot((lax.div(col, NV) == at) & (lax.rem(col, NV) == lax.div(row, PAD)))
    latitude = me * ROWS + lax.div(iota((ROWS * NV, 128), 0), NV)
    latitude = jnp.minimum(latitude, NT - 1 - latitude)
    over = jnp.where(lon[...] > 512 * (((latitude + EDGE) >> 7) + 1), 1.0, 0.0)
    over = jnp.broadcast_to(jnp.max(over, axis=0, keepdims=True), (PAD - ROWS, 128))
    flag_ref[...] = over
    folded[...] = jnp.zeros_like(folded)
    edges[...] = jnp.zeros_like(edges)

    lane_block = lax.div(iota((PAD, 128), 1), 16)

    def fourier(r):
        odd = lax.rem(r, 2)
        first = dot(x[:, :, : NLON // 2].reshape(ROWS * NV, NLON // 2), basis[r])
        second = dot(x[:, :, NLON // 2 :].reshape(ROWS * NV, NLON // 2), basis[r])
        values = first + second * jnp.where((iota((1, 2 * WAVES), 1) >> 8) == odd, 1.0, -1.0)
        column = iota((8, 2 * WAVES), 1)
        column = 2 * (column & 127) + (column >> 8)
        waves = r * WAVES + jnp.where(odd == 1, WAVES - 1 - column, column)
        twice = jnp.broadcast_to(2 * waves[:1], (ROWS * NV, 2 * WAVES))
        longitudes = jnp.concatenate([lon[...]] * 4, axis=1)
        values = jnp.where(twice < longitudes, values, 0.0).astype(BF16)
        values = dot(order[...], values).astype(BF16)
        values = dot(values, route[...])
        for high in range(LATS // 8):
            blocks = []
            for v in range(NV):
                block = values[v * PAD : (v + 1) * PAD, high * 128 : (high + 1) * 128]
                blocks.append(pltpu.roll(block, 16 * v, 1) if v else block)
            for bit in range(3):
                taken = (lane_block >> bit) & 1 == 1
                blocks = [jnp.where(taken, blocks[(i + (1 << bit)) % 8], blocks[i]) for i in range(8)]
            for low in range(8):
                block = jnp.concatenate([blocks[-low % 8][:ROWS], over], axis=0)
                sent[r, high * 8 + low] = block.astype(BF16)

    def send_lat(r):
        group = jnp.where((r == 0) & (pair < POLAR), ROUNDS, r) if plan.sparse else r

        def start(k, carry):
            peer = lax.rem(me + k, LATS)
            pltpu.make_async_remote_copy(
                src_ref=sent.at[r, peer],
                dst_ref=got.at[r, me],
                send_sem=lat_send.at[r],
                recv_sem=lat_recv.at[group],
                device_id=(peer, lev),
                device_id_type=MESH,
            ).start()
            return carry

        lax.fori_loop(1, LATS, start, 0)

    def send_lev(source, place, send, recv):
        def start(k, carry):
            peer = lax.rem(lev + k, LEVS)
            pltpu.make_async_remote_copy(
                src_ref=source.at[peer],
                dst_ref=place.at[lev],
                send_sem=send,
                recv_sem=recv,
                device_id=(me, peer),
                device_id_type=MESH,
            ).start()
            return carry

        lax.fori_loop(1, LEVS, start, 0)

    def turn(chunk):
        r, low, high = plan.chunks[chunk]
        first, last = plan.sources(chunk)
        group = ROUNDS if plan.sparse and chunk == 0 else r
        mine = (pair >= first) & (pair < last)
        messages = 2 * (last - first)

        @pl.when(mine)
        def _():
            await_bytes(got.at[r, pl.ds(0, messages - 1)], lat_recv.at[group])
            got[r, me] = sent[r, me]

        if messages < LATS:

            @pl.when(jnp.logical_not(mine))
            def _():
                await_bytes(got.at[r, pl.ds(0, messages)], lat_recv.at[group])

        for i in plan.pairs(chunk):
            north = got[r, i].astype(F32)
            south = got[r, LATS - 1 - i].astype(F32)
            folded[0, pl.ds(i * ROWS, ROWS), :] = north[:ROWS] + south[:ROWS]
            folded[1, pl.ds(i * ROWS, ROWS), :] = north[:ROWS] - south[:ROWS]
            if r == 0:
                flag_ref[...] = jnp.maximum(flag_ref[...], jnp.maximum(north[ROWS:], south[ROWS:]))
        row = iota((128, 128), 0)
        col = iota((128, 128), 1)
        source = 16 * (((row & 7) + me) & 7) + 8 * ((row >> 3) & 1) + (row >> 4)
        pick = one_hot(col == source)
        for part in range(2):
            values = dot_nt(pick, folded[part, low:high].astype(BF16)).astype(BF16)
            turned[chunk][part] = values.reshape(LEVS, 16, high - low)
            send_lev(turned[chunk].at[part], ready[chunk].at[part], lev_send.at[chunk, part], lev_recv.at[chunk, part])
        if plan.sparse and r:
            for part in range(2):
                values = dot_nt(pick, folded[part, low - 128 : low].astype(BF16))
                block = 2 * (r - 1) + part
                values = pltpu.roll(values, (EDGE * block + EDGE) % 128, 1)
                edges[...] = jnp.where((col >> 4) == block, values, edges[...])
            if r == 1:
                edge_sent[...] = edges[...].astype(BF16).reshape(LEVS, 16, 128)
                send_lev(edge_sent, edge_got, edge_send, edge_recv)

    def vertical_operator():
        pick_out = one_hot(iota((128, 64), 1) == (iota((128, 64), 0) >> 1))
        col = iota((64, 128), 1)
        pick_in = one_hot(iota((64, 128), 0) == 8 * (col >> 4) + (col & 7))
        same = (iota((128, 128), 0) & 1) == ((iota((128, 128), 1) >> 3) & 1)
        whole = vertical_ref[...]
        high = whole.astype(BF16)
        low = (whole - high.astype(F32)).astype(BF16)
        for k, term in enumerate((high, low)):
            term = dot_nt(pick_out, term).astype(BF16)
            term = dot(term, pick_in)
            mix[:, pl.ds(128 * k, 128)] = jnp.where(same, term, 0.0).astype(BF16)

    def mixed(values):
        values = values.reshape(128, values.shape[-1])
        return dot(mix[...], jnp.concatenate([values, values], axis=0))

    def received(chunk, part):
        await_bytes(ready[chunk].at[part, pl.ds(0, LEVS - 1)], lev_recv.at[chunk, part])
        ready[chunk][part, lev] = turned[chunk][part, lev]
        return mixed(ready[chunk][part]).astype(BF16)

    def legendre(r, edge):
        width = HALF - 128 * r
        wave = wave_ref[(me * LEVS + lev) * ROUNDS + r]
        for part in range(2):
            pieces = [received(k, part) for k in range(count) if plan.chunks[k][0] == r]
            if edge is not None and r:
                block = 2 * (r - 1) + part
                piece = pltpu.roll(edge, (128 - EDGE - EDGE * block) % 128, 1)
                pieces.insert(0, jnp.where(iota((128, 128), 1) >= 128 - EDGE, piece, 0.0).astype(BF16))
            values = jnp.concatenate(pieces, axis=1) if len(pieces) > 1 else pieces[0]
            table_copies[r, part].wait()
            start = plan.table_start(r)
            total = dot(values, table[r, start:, pl.ds(part * HALF, width)])
            degree = wave + 2 * iota((128, width), 1) + part
            total = jnp.where(degree < NT, total, 0.0)
            result[r, :, :, pl.ds(part * HALF, width)] = total.reshape(64, 2, width)
            if width < HALF:
                result[r, :, :, pl.ds(part * HALF + width, HALF - width)] = jnp.zeros((64, 2, HALF - width), F32)
        pltpu.make_async_copy(result.at[r], out_ref.at[:, r], out_sem.at[r]).start()

    grid_copy.wait()

    def advance(step, carry):
        r, due = round_at(step)

        @pl.when(due)
        def _():
            basis_copy(r).wait()
            fourier(r)

        @pl.when(step == 0)
        def _():
            pl.semaphore_wait(barrier, LATS - 1 + LEVS - 1)

        @pl.when(due)
        def _():
            send_lat(r)

        @pl.when(step == 0)
        def _():
            vertical_operator()

        for chunk in range(count):

            @pl.when(step == plan.turn_step[chunk])
            def _():
                turn(chunk)

        return carry

    lax.fori_loop(0, ROUNDS + 1, advance, 0)
    edge = None
    if plan.sparse:
        await_bytes(edge_got.at[pl.ds(0, LEVS - 1)], edge_recv)
        edge_got[lev] = edge_sent[lev]
        edge = mixed(edge_got[...])
    for r in reversed(range(ROUNDS)):
        legendre(r, edge)
    for r in range(ROUNDS):
        pltpu.make_async_copy(result.at[r], out_ref.at[:, r], out_sem.at[r]).wait()

    def drain_lat(r, carry):
        @pl.when(sends(r))
        def _():
            await_bytes(sent.at[r, pl.ds(0, LATS - 1)], lat_send.at[r])

        return carry

    lax.fori_loop(0, ROUNDS, drain_lat, 0)
    for chunk in range(count):
        for part in range(2):
            await_bytes(turned[chunk].at[part, pl.ds(0, LEVS - 1)], lev_send.at[chunk, part])
    if plan.sparse:
        await_bytes(edge_sent.at[pl.ds(0, LEVS - 1)], edge_send)


def transform(plan, collective_id, wave_table, wave_row, lon_count, vertical, grid_field, basis, legendre):
    anywhere = pl.BlockSpec(memory_space=pl.ANY)
    vmem = pl.BlockSpec(memory_space=pltpu.VMEM)
    smem = pl.BlockSpec(memory_space=pltpu.SMEM)
    count = len(plan.chunks)
    chunk_shapes = [pltpu.VMEM((2, LEVS, 16, high - low), BF16) for _, low, high in plan.chunks]
    return pl.pallas_call(
        functools.partial(kernel, plan),
        out_shape=[
            jax.ShapeDtypeStruct((64, ROUNDS, 2, NT), F32),
            jax.ShapeDtypeStruct((PAD - ROWS, 128), F32),
        ],
        in_specs=[smem, smem, vmem, vmem, anywhere, anywhere, anywhere],
        out_specs=[anywhere, vmem],
        scratch_shapes=[
            pltpu.VMEM((ROWS, NV, NLON), BF16),
            pltpu.VMEM((ROUNDS, NLON // 2, 2 * WAVES), BF16),
            pltpu.VMEM((ROUNDS, HALF, NT), BF16),
            pltpu.VMEM((ROWS * NV, 128), jnp.int32),
            pltpu.VMEM((2 * WAVES, 2 * WAVES), BF16),
            pltpu.VMEM((NV * PAD, ROWS * NV), BF16),
            pltpu.VMEM((128, 256), BF16),
            pltpu.VMEM((2, HALF, 128), F32),
            pltpu.VMEM((128, 128), F32),
            pltpu.VMEM((ROUNDS, LATS, PAD, 128), BF16),
            pltpu.VMEM((ROUNDS, LATS, PAD, 128), BF16),
            pltpu.VMEM((LEVS, 16, 128), BF16),
            pltpu.VMEM((LEVS, 16, 128), BF16),
            pltpu.VMEM((ROUNDS, 64, 2, NT), F32),
            *chunk_shapes,
            *chunk_shapes,
            pltpu.SemaphoreType.DMA,
            pltpu.SemaphoreType.DMA((ROUNDS,)),
            pltpu.SemaphoreType.DMA((ROUNDS, 2)),
            pltpu.SemaphoreType.DMA((ROUNDS,)),
            pltpu.SemaphoreType.DMA((ROUNDS,)),
            pltpu.SemaphoreType.DMA((ROUNDS + 1,)),
            pltpu.SemaphoreType.DMA((count, 2)),
            pltpu.SemaphoreType.DMA((count, 2)),
            pltpu.SemaphoreType.DMA,
            pltpu.SemaphoreType.DMA,
        ],
        compiler_params=pltpu.CompilerParams(
            collective_id=collective_id, has_side_effects=True, vmem_limit_bytes=56 << 20
        ),
        cost_estimate=pl.CostEstimate(flops=6_000_000_000, bytes_accessed=24_000_000, transcendentals=0),
    )(wave_table, lon_count, wave_row, vertical, grid_field, basis, legendre)


def on_device(grid_field, lon_count, wave_table, legendre, vertical):
    basis = jnp.asarray(basis_constant())
    args = (wave_table, wave_table.reshape(1, NT), lon_count, vertical, grid_field, basis, legendre)
    spectral, flag = transform(Plan(True), 0, *args)
    spectral = lax.cond(
        flag[0, 0] > 0, lambda kept, *rest: transform(Plan(False), 1, *rest)[0], lambda kept, *rest: kept, spectral, *args
    )
    return spectral.transpose(0, 2, 1, 3)


def solution(mesh):
    return jax.shard_map(
        on_device,
        mesh=mesh,
        in_specs=(P("lat", "lev", None), P("lat"), P(), P(("lat", "lev"), None, None), P()),
        out_specs=P(None, None, ("lat", "lev"), None),
        check_vma=False,
    )
```

```python
import functools
import math

import jax
import jax.numpy as jnp
import ml_dtypes
import numpy as np
from jax import lax
from jax.experimental import pallas as pl
from jax.experimental.pallas import tpu as pltpu
from jax.sharding import PartitionSpec as P

MESH = pl.DeviceIdType.MESH
NLON = 2560
NT = 1280
HALF = 640
ROUNDS = 5
WAVES = 256
LATS = 32
LEVS = 8
ROWS = 40
PAD = 48
NV = 8
EDGE = 16
POLAR = 7
F32 = jnp.float32
BF16 = jnp.bfloat16
PEERS = (16, 2, 8, 4, 24, 6, 1, 18, 10, 20, 26, 12, 28, 14, 30, 22, 17, 3, 9, 5, 25, 7, 19, 11, 21, 27, 13, 29, 15, 31, 23)


class Plan:
    def __init__(self, sparse):
        self.sparse = sparse
        if sparse:
            self.first_pair = [0] + [(128 * r - EDGE) // ROWS for r in range(1, ROUNDS)]
            self.chunks = [(0, 0, 256), (3, 384, HALF), (2, 256, HALF), (1, 128, HALF), (0, 256, HALF), (4, 512, HALF)]
            self.turn_step = [2, 2, 3, 4, 5, 6]
            self.sums = (3, 2, 1, 0, 4)
        else:
            self.first_pair = [0] * ROUNDS
            self.chunks = [(r, 0, HALF) for r in range(ROUNDS)]
            self.turn_step = [r + 1 for r in range(ROUNDS)]
            self.sums = tuple(range(ROUNDS))

    def pairs(self, chunk):
        r, low, high = self.chunks[chunk]
        edge = EDGE if self.sparse and r else 0
        return range((low - edge) // ROWS, -(-high // ROWS))

    def sources(self, chunk):
        r = self.chunks[chunk][0]
        if self.sparse and r == 0:
            return (0, POLAR) if chunk == 0 else (POLAR, LATS // 2)
        return (self.first_pair[r], LATS // 2)

    def table_start(self, r):
        return 128 * max(r - 1, 0) if self.sparse else 0


def basis_constant():
    points = np.arange(NLON // 2, dtype=np.int64)
    column = np.arange(WAVES, dtype=np.int64)
    factor = np.float32(math.sqrt(2.0 / NLON))
    rounds = []
    for r in range(ROUNDS):
        waves = r * WAVES + (column if r % 2 == 0 else WAVES - 1 - column)
        phases = points[:, None] * waves[None, :] % NLON
        angles = phases.astype(np.float32) * np.float32(2.0 * math.pi / NLON)
        cosines, sines = np.cos(angles) * factor, -np.sin(angles) * factor
        rounds.append(np.concatenate([cosines[:, 0::2], sines[:, 0::2], cosines[:, 1::2], sines[:, 1::2]], axis=1))
    return np.stack(rounds).astype(ml_dtypes.bfloat16)


def iota(shape, dim):
    return lax.broadcasted_iota(jnp.int32, shape, dim)


def one_hot(mask):
    return jnp.where(mask, 1.0, 0.0).astype(BF16)


def dot(a, b):
    return jnp.dot(a, b, preferred_element_type=F32)


def dot_nt(a, b):
    return lax.dot_general(a, b, (((1,), (1,)), ((), ())), preferred_element_type=F32)


def await_bytes(ref, semaphore):
    pltpu.make_async_copy(ref, ref, semaphore).wait()


def kernel(plan, *refs):
    (
        wave_ref, lon_ref, wave_row_ref, vertical_ref, grid_ref, basis_ref, legendre_ref,
        out_ref, flag_out,
        x, flag_ref, basis, table, lon, route, order, mix, folded, edges, sent, got, edge_sent, edge_got, result, *chunk_refs,
    ) = refs
    count = len(plan.chunks)
    turned, ready = chunk_refs[:count], chunk_refs[count : 2 * count]
    (
        in_sem, basis_sem, table_sem, out_sem, lat_send, lat_recv, lev_send, lev_recv, edge_send, edge_recv,
    ) = chunk_refs[2 * count :]
    me = lax.axis_index("lat")
    lev = lax.axis_index("lev")
    pair = jnp.minimum(me, LATS - 1 - me)

    def sends(r):
        first = 0
        for k in range(1, ROUNDS):
            first = jnp.where(r == k, plan.first_pair[k], first)
        return pair >= first

    def round_at(step):
        if not plan.sparse:
            return step, step < ROUNDS
        usual = jnp.where(step == ROUNDS - 1, ROUNDS - 1, ROUNDS - 2 - step)
        early = (pair < POLAR) & (step == 0)
        r = jnp.where(early, 0, usual)
        due = early | ((step > 0) | (pair >= POLAR)) & sends(usual) & ~((pair < POLAR) & (usual == 0))
        return jnp.maximum(r, 0), due & (step < ROUNDS)

    def basis_copy(r):
        return pltpu.make_async_copy(basis_ref.at[r], basis.at[r], basis_sem.at[r])

    grid_copy = pltpu.make_async_copy(grid_ref, x, in_sem)
    grid_copy.start()

    def start_basis(step, carry):
        r, due = round_at(step)

        @pl.when(due)
        def _():
            basis_copy(r).start()

        return carry

    lax.fori_loop(0, ROUNDS, start_basis, 0)
    table_copies = {}
    for r in reversed(range(ROUNDS)):
        start, width = plan.table_start(r), HALF - 128 * r
        for part in range(2):
            block = (r, pl.ds(start, HALF - start), pl.ds(part * HALF, width))
            copy = pltpu.make_async_copy(legendre_ref.at[block], table.at[block], table_sem.at[r, part])
            copy.start()
            table_copies[r, part] = copy

    barrier = pltpu.get_barrier_semaphore()

    def greet_lat(k, carry):
        pl.semaphore_signal(barrier, inc=1, device_id=(lax.rem(me + k, LATS), lev), device_id_type=MESH)
        return carry

    def greet_lev(k, carry):
        pl.semaphore_signal(barrier, inc=1, device_id=(me, lax.rem(lev + k, LEVS)), device_id_type=MESH)
        return carry

    lax.fori_loop(1, LATS, greet_lat, 0)
    lax.fori_loop(1, LEVS, greet_lev, 0)

    for t in range(ROWS):
        lon[pl.ds(t * NV, NV), :] = jnp.full((NV, 128), lon_ref[t], jnp.int32)
    row = iota((NT, 2 * WAVES), 0)
    col = iota((NT, 2 * WAVES), 1)
    pick = one_hot(row == ROUNDS * (8 * (col >> 4) + (col & 7)))
    waves = jnp.broadcast_to(wave_row_ref[...].reshape(1, NT).astype(F32), (8, NT)).astype(BF16)
    place = dot(waves, pick).astype(jnp.int32)
    target = WAVES * (place & 1) + 128 * ((iota((8, 2 * WAVES), 1) >> 3) & 1) + (place >> 1)
    route[...] = one_hot(iota((2 * WAVES, 2 * WAVES), 0) == target[:1])
    row = iota((NV * PAD, ROWS * NV), 0)
    col = iota((NV * PAD, ROWS * NV), 1)
    at = lax.rem(row, PAD)
    at = jnp.where(me < LATS // 2, at, ROWS - 1 - at)
    order[...] = one_hot((lax.div(col, NV) == at) & (lax.rem(col, NV) == lax.div(row, PAD)))
    latitude = me * ROWS + lax.div(iota((ROWS * NV, 128), 0), NV)
    latitude = jnp.minimum(latitude, NT - 1 - latitude)
    over = jnp.where(lon[...] > 512 * (((latitude + EDGE) >> 7) + 1), 1.0, 0.0)
    over = jnp.broadcast_to(jnp.max(over, axis=0, keepdims=True), (PAD - ROWS, 128))
    flag_ref[...] = over
    folded[...] = jnp.zeros_like(folded)
    edges[...] = jnp.zeros_like(edges)

    lane_block = lax.div(iota((PAD, 128), 1), 16)

    def fourier(r):
        odd = lax.rem(r, 2)
        first = dot(x[:, :, : NLON // 2].reshape(ROWS * NV, NLON // 2), basis[r])
        second = dot(x[:, :, NLON // 2 :].reshape(ROWS * NV, NLON // 2), basis[r])
        values = first + second * jnp.where((iota((1, 2 * WAVES), 1) >> 8) == odd, 1.0, -1.0)
        column = iota((8, 2 * WAVES), 1)
        column = 2 * (column & 127) + (column >> 8)
        waves = r * WAVES + jnp.where(odd == 1, WAVES - 1 - column, column)
        twice = jnp.broadcast_to(2 * waves[:1], (ROWS * NV, 2 * WAVES))
        longitudes = jnp.concatenate([lon[...]] * 4, axis=1)
        values = jnp.where(twice < longitudes, values, 0.0).astype(BF16)
        values = dot(order[...], values).astype(BF16)
        values = dot(values, route[...])
        for high in range(LATS // 8):
            blocks = []
            for v in range(NV):
                block = values[v * PAD : (v + 1) * PAD, high * 128 : (high + 1) * 128]
                blocks.append(pltpu.roll(block, 16 * v, 1) if v else block)
            for bit in range(3):
                taken = (lane_block >> bit) & 1 == 1
                blocks = [jnp.where(taken, blocks[(i + (1 << bit)) % 8], blocks[i]) for i in range(8)]
            for low in range(8):
                block = jnp.concatenate([blocks[-low % 8][:ROWS], over], axis=0)
                sent[r, high * 8 + low] = block.astype(BF16)

    def send_lat(r):
        group = jnp.where((r == 0) & (pair < POLAR), ROUNDS, r) if plan.sparse else r

        for k in PEERS:
            peer = me ^ k
            pltpu.make_async_remote_copy(
                src_ref=sent.at[r, peer],
                dst_ref=got.at[r, me],
                send_sem=lat_send.at[r],
                recv_sem=lat_recv.at[group],
                device_id=(peer, lev),
                device_id_type=MESH,
            ).start()

    def send_lev(source, place, send, recv):
        for k in (4, 3, 5, 2, 6, 1, 7):
            peer = (lev + k) & (LEVS - 1)
            pltpu.make_async_remote_copy(
                src_ref=source.at[peer],
                dst_ref=place.at[lev],
                send_sem=send,
                recv_sem=recv,
                device_id=(me, peer),
                device_id_type=MESH,
            ).start()

    def edge_place(r, part):
        return (1, part) if r == 4 else (0, 2 * (r - 1) + part)

    def turn(chunk):
        r, low, high = plan.chunks[chunk]
        first, last = plan.sources(chunk)
        group = ROUNDS if plan.sparse and chunk == 0 else r
        mine = (pair >= first) & (pair < last)
        messages = 2 * (last - first)

        @pl.when(mine)
        def _():
            await_bytes(got.at[r, pl.ds(0, messages - 1)], lat_recv.at[group])
            got[r, me] = sent[r, me]

        if messages < LATS:

            @pl.when(jnp.logical_not(mine))
            def _():
                await_bytes(got.at[r, pl.ds(0, messages)], lat_recv.at[group])

        for i in plan.pairs(chunk):
            north = got[r, i].astype(F32)
            south = got[r, LATS - 1 - i].astype(F32)
            folded[0, pl.ds(i * ROWS, ROWS), :] = north[:ROWS] + south[:ROWS]
            folded[1, pl.ds(i * ROWS, ROWS), :] = north[:ROWS] - south[:ROWS]
            if r == 0:
                flag_ref[...] = jnp.maximum(flag_ref[...], jnp.maximum(north[ROWS:], south[ROWS:]))
        row = iota((128, 128), 0)
        col = iota((128, 128), 1)
        source = 16 * (((row & 7) + me) & 7) + 8 * ((row >> 3) & 1) + (row >> 4)
        pick = one_hot(col == source)
        for part in range(2):
            values = dot_nt(pick, folded[part, low:high].astype(BF16)).astype(BF16)
            turned[chunk][part] = values.reshape(LEVS, 16, high - low)
            send_lev(turned[chunk].at[part], ready[chunk].at[part], lev_send.at[chunk, part], lev_recv.at[chunk, part])
        if plan.sparse and r:
            for part in range(2):
                values = dot_nt(pick, folded[part, low - 128 : low].astype(BF16))
                tile, block = edge_place(r, part)
                values = pltpu.roll(values, (EDGE * block + EDGE) % 128, 1)
                edges[tile] = jnp.where((col >> 4) == block, values, edges[tile])
            if r in (1, 4):
                edge_sent[tile] = edges[tile].astype(BF16).reshape(LEVS, 16, 128)
                send_lev(edge_sent.at[tile], edge_got.at[tile], edge_send.at[tile], edge_recv.at[tile])

    def vertical_operator():
        pick_out = one_hot(iota((128, 64), 1) == (iota((128, 64), 0) >> 1))
        col = iota((64, 128), 1)
        pick_in = one_hot(iota((64, 128), 0) == 8 * (col >> 4) + (col & 7))
        same = (iota((128, 128), 0) & 1) == ((iota((128, 128), 1) >> 3) & 1)
        whole = vertical_ref[...]
        high = whole.astype(BF16)
        low = (whole - high.astype(F32)).astype(BF16)
        for k, term in enumerate((high, low)):
            term = dot_nt(pick_out, term).astype(BF16)
            term = dot(term, pick_in)
            mix[:, pl.ds(128 * k, 128)] = jnp.where(same, term, 0.0).astype(BF16)

    def mixed(values):
        values = values.reshape(128, values.shape[-1])
        return dot(mix[...], jnp.concatenate([values, values], axis=0))

    def received(chunk, part):
        await_bytes(ready[chunk].at[part, pl.ds(0, LEVS - 1)], lev_recv.at[chunk, part])
        ready[chunk][part, lev] = turned[chunk][part, lev]
        return mixed(ready[chunk][part]).astype(BF16)

    edge_values = {}

    def edge_piece(r, part):
        tile, block = edge_place(r, part)
        if tile not in edge_values:
            await_bytes(edge_got.at[tile, pl.ds(0, LEVS - 1)], edge_recv.at[tile])
            edge_got[tile, lev] = edge_sent[tile, lev]
            edge_values[tile] = mixed(edge_got[tile])
        piece = pltpu.roll(edge_values[tile], (128 - EDGE - EDGE * block) % 128, 1)
        return jnp.where(iota((128, 128), 1) >= 128 - EDGE, piece, 0.0).astype(BF16)

    def legendre(r):
        width = HALF - 128 * r
        wave = wave_ref[(me * LEVS + lev) * ROUNDS + r]
        for part in range(2):
            pieces = [received(k, part) for k in range(count) if plan.chunks[k][0] == r]
            if plan.sparse and r:
                pieces.insert(0, edge_piece(r, part))
            values = jnp.concatenate(pieces, axis=1) if len(pieces) > 1 else pieces[0]
            table_copies[r, part].wait()
            start = plan.table_start(r)
            total = dot(values, table[r, start:, pl.ds(part * HALF, width)])
            degree = wave + 2 * iota((128, width), 1) + part
            total = jnp.where(degree < NT, total, 0.0)
            result[r, :, :, pl.ds(part * HALF, width)] = total.reshape(64, 2, width)
            if width < HALF:
                result[r, :, :, pl.ds(part * HALF + width, HALF - width)] = jnp.zeros((64, 2, HALF - width), F32)
        pltpu.make_async_copy(result.at[r], out_ref.at[:, r], out_sem.at[r]).start()

    grid_copy.wait()

    def advance(step, carry):
        r, due = round_at(step)

        @pl.when(due)
        def _():
            basis_copy(r).wait()
            fourier(r)

        @pl.when(step == 0)
        def _():
            pl.semaphore_wait(barrier, LATS - 1 + LEVS - 1)

        @pl.when(due)
        def _():
            send_lat(r)

        @pl.when(step == 0)
        def _():
            vertical_operator()

        for chunk in range(count):

            @pl.when(step == plan.turn_step[chunk])
            def _():
                turn(chunk)

        return carry

    lax.fori_loop(0, max(plan.turn_step) + 1, advance, 0)
    flag_out[0] = (jnp.max(flag_ref[...]) > 0).astype(jnp.int32)
    for r in plan.sums:
        legendre(r)
    for r in range(ROUNDS):
        pltpu.make_async_copy(result.at[r], out_ref.at[:, r], out_sem.at[r]).wait()

    def drain_lat(r, carry):
        @pl.when(sends(r))
        def _():
            await_bytes(sent.at[r, pl.ds(0, LATS - 1)], lat_send.at[r])

        return carry

    lax.fori_loop(0, ROUNDS, drain_lat, 0)
    for chunk in range(count):
        for part in range(2):
            await_bytes(turned[chunk].at[part, pl.ds(0, LEVS - 1)], lev_send.at[chunk, part])
    if plan.sparse:
        for tile in range(2):
            await_bytes(edge_sent.at[tile, pl.ds(0, LEVS - 1)], edge_send.at[tile])


def transform(plan, collective_id, wave_table, wave_row, lon_count, vertical, grid_field, basis, legendre):
    anywhere = pl.BlockSpec(memory_space=pl.ANY)
    vmem = pl.BlockSpec(memory_space=pltpu.VMEM)
    smem = pl.BlockSpec(memory_space=pltpu.SMEM)
    count = len(plan.chunks)
    chunk_shapes = [pltpu.VMEM((2, LEVS, 16, high - low), BF16) for _, low, high in plan.chunks]
    return pl.pallas_call(
        functools.partial(kernel, plan),
        out_shape=[
            jax.ShapeDtypeStruct((64, ROUNDS, 2, NT), F32),
            jax.ShapeDtypeStruct((1,), jnp.int32),
        ],
        in_specs=[smem, smem, vmem, vmem, anywhere, anywhere, anywhere],
        out_specs=[anywhere, smem],
        scratch_shapes=[
            pltpu.VMEM((ROWS, NV, NLON), BF16),
            pltpu.VMEM((PAD - ROWS, 128), F32),
            pltpu.VMEM((ROUNDS, NLON // 2, 2 * WAVES), BF16),
            pltpu.VMEM((ROUNDS, HALF, NT), BF16),
            pltpu.VMEM((ROWS * NV, 128), jnp.int32),
            pltpu.VMEM((2 * WAVES, 2 * WAVES), BF16),
            pltpu.VMEM((NV * PAD, ROWS * NV), BF16),
            pltpu.VMEM((128, 256), BF16),
            pltpu.VMEM((2, HALF, 128), F32),
            pltpu.VMEM((2, 128, 128), F32),
            pltpu.VMEM((ROUNDS, LATS, PAD, 128), BF16),
            pltpu.VMEM((ROUNDS, LATS, PAD, 128), BF16),
            pltpu.VMEM((2, LEVS, 16, 128), BF16),
            pltpu.VMEM((2, LEVS, 16, 128), BF16),
            pltpu.VMEM((ROUNDS, 64, 2, NT), F32),
            *chunk_shapes,
            *chunk_shapes,
            pltpu.SemaphoreType.DMA,
            pltpu.SemaphoreType.DMA((ROUNDS,)),
            pltpu.SemaphoreType.DMA((ROUNDS, 2)),
            pltpu.SemaphoreType.DMA((ROUNDS,)),
            pltpu.SemaphoreType.DMA((ROUNDS,)),
            pltpu.SemaphoreType.DMA((ROUNDS + 1,)),
            pltpu.SemaphoreType.DMA((count, 2)),
            pltpu.SemaphoreType.DMA((count, 2)),
            pltpu.SemaphoreType.DMA((2,)),
            pltpu.SemaphoreType.DMA((2,)),
        ],
        compiler_params=pltpu.CompilerParams(
            collective_id=collective_id, has_side_effects=True, vmem_limit_bytes=56 << 20
        ),
        cost_estimate=pl.CostEstimate(flops=6_000_000_000, bytes_accessed=24_000_000, transcendentals=0),
    )(wave_table, lon_count, wave_row, vertical, grid_field, basis, legendre)


def on_device(grid_field, lon_count, wave_table, legendre, vertical):
    basis = jnp.asarray(basis_constant())
    args = (wave_table, wave_table, lon_count, vertical, grid_field, basis, legendre)
    spectral, flag = transform(Plan(True), 0, *args)
    spectral = lax.cond(
        flag[0] > 0, lambda kept, *rest: transform(Plan(False), 1, *rest)[0], lambda kept, *rest: kept, spectral, *args
    )
    return spectral.transpose(0, 2, 1, 3)


def solution(mesh):
    return jax.shard_map(
        on_device,
        mesh=mesh,
        in_specs=(P("lat", "lev", None), P("lat"), P(), P(("lat", "lev"), None, None), P()),
        out_specs=P(None, None, ("lat", "lev"), None),
        check_vma=False,
    )
```

```python
import functools
import math

import jax
import jax.numpy as jnp
import ml_dtypes
import numpy as np
from jax import lax
from jax.experimental import pallas as pl
from jax.experimental.pallas import tpu as pltpu
from jax.sharding import PartitionSpec as P

MESH = pl.DeviceIdType.MESH
NLON = 2560
NT = 1280
HALF = 640
ROUNDS = 5
WAVES = 256
LATS = 32
LEVS = 8
ROWS = 40
PAD = 48
NV = 8
EDGE = 16
POLAR = 7
F32 = jnp.float32
BF16 = jnp.bfloat16
PEERS = (29, 18, 12, 11, 27, 2, 6, 31, 8, 17, 10, 20, 30, 14, 22, 1, 21, 24, 7, 13, 23, 15, 16, 4, 9, 3, 25, 26, 28, 19, 5)


class Plan:
    def __init__(self, sparse):
        self.sparse = sparse
        if sparse:
            self.first_pair = [0] + [(128 * r - EDGE) // ROWS for r in range(1, ROUNDS)]
            self.chunks = [(0, 0, 256), (3, 384, HALF), (2, 256, HALF), (1, 128, HALF), (0, 256, HALF), (4, 512, HALF)]
            self.turn_step = [3, 3, 4, 5, 6, 7]
            self.sums = (3, 2, 1, 0, 4)
        else:
            self.first_pair = [0] * ROUNDS
            self.chunks = [(r, 0, HALF) for r in range(ROUNDS)]
            self.turn_step = [r + 1 for r in range(ROUNDS)]
            self.sums = tuple(range(ROUNDS))

    def pairs(self, chunk):
        r, low, high = self.chunks[chunk]
        edge = EDGE if self.sparse and r else 0
        return range((low - edge) // ROWS, -(-high // ROWS))

    def sources(self, chunk):
        r = self.chunks[chunk][0]
        if self.sparse and r == 0:
            return (0, POLAR) if chunk == 0 else (POLAR, LATS // 2)
        return (self.first_pair[r], LATS // 2)

    def table_start(self, r):
        return 128 * max(r - 1, 0) if self.sparse else 0


def basis_constant():
    points = np.arange(NLON // 2, dtype=np.int64)
    column = np.arange(WAVES, dtype=np.int64)
    factor = np.float32(math.sqrt(2.0 / NLON))
    rounds = []
    for r in range(ROUNDS):
        waves = r * WAVES + (column if r % 2 == 0 else WAVES - 1 - column)
        phases = points[:, None] * waves[None, :] % NLON
        angles = phases.astype(np.float32) * np.float32(2.0 * math.pi / NLON)
        cosines, sines = np.cos(angles) * factor, -np.sin(angles) * factor
        rounds.append(np.concatenate([cosines[:, 0::2], sines[:, 0::2], cosines[:, 1::2], sines[:, 1::2]], axis=1))
    return np.stack(rounds).astype(ml_dtypes.bfloat16)


def iota(shape, dim):
    return lax.broadcasted_iota(jnp.int32, shape, dim)


def one_hot(mask):
    return jnp.where(mask, 1.0, 0.0).astype(BF16)


def dot(a, b):
    return jnp.dot(a, b, preferred_element_type=F32)


def dot_nt(a, b):
    return lax.dot_general(a, b, (((1,), (1,)), ((), ())), preferred_element_type=F32)


def await_bytes(ref, semaphore):
    pltpu.make_async_copy(ref, ref, semaphore).wait()


def kernel(plan, *refs):
    (
        wave_ref, lon_ref, wave_row_ref, vertical_ref, grid_ref, basis_ref, legendre_ref,
        out_ref, flag_out,
        x, flag_ref, basis, table, lon, route, order, mix, folded, edges, sent, got, edge_sent, edge_got, result, *chunk_refs,
    ) = refs
    count = len(plan.chunks)
    turned, ready = chunk_refs[:count], chunk_refs[count : 2 * count]
    (
        in_sem, basis_sem, table_sem, out_sem, lat_send, lat_recv, lev_send, lev_recv, edge_send, edge_recv,
    ) = chunk_refs[2 * count :]
    me = lax.axis_index("lat")
    lev = lax.axis_index("lev")
    pair = jnp.minimum(me, LATS - 1 - me)

    def sends(r):
        first = 0
        for k in range(1, ROUNDS):
            first = jnp.where(r == k, plan.first_pair[k], first)
        return pair >= first

    def round_at(step):
        if not plan.sparse:
            return step, step < ROUNDS
        usual = jnp.where(step == ROUNDS - 1, ROUNDS - 1, ROUNDS - 2 - step)
        early = (pair < POLAR) & (step == 0)
        r = jnp.where(early, 0, usual)
        due = early | ((step > 0) | (pair >= POLAR)) & sends(usual) & ~((pair < POLAR) & (usual == 0))
        return jnp.maximum(r, 0), due & (step < ROUNDS)

    def basis_copy(r):
        return pltpu.make_async_copy(basis_ref.at[r], basis.at[r], basis_sem.at[r])

    grid_copy = pltpu.make_async_copy(grid_ref, x, in_sem)
    grid_copy.start()

    def start_basis(step, carry):
        r, due = round_at(step)

        @pl.when(due)
        def _():
            basis_copy(r).start()

        return carry

    lax.fori_loop(0, ROUNDS, start_basis, 0)
    table_copies = {}
    for r in reversed(range(ROUNDS)):
        start, width = plan.table_start(r), HALF - 128 * r
        for part in range(2):
            block = (r, pl.ds(start, HALF - start), pl.ds(part * HALF, width))
            copy = pltpu.make_async_copy(legendre_ref.at[block], table.at[block], table_sem.at[r, part])
            copy.start()
            table_copies[r, part] = copy

    barrier = pltpu.get_barrier_semaphore()

    def greet_lat(k, carry):
        pl.semaphore_signal(barrier, inc=1, device_id=(lax.rem(me + k, LATS), lev), device_id_type=MESH)
        return carry

    def greet_lev(k, carry):
        pl.semaphore_signal(barrier, inc=1, device_id=(me, lax.rem(lev + k, LEVS)), device_id_type=MESH)
        return carry

    lax.fori_loop(1, LATS, greet_lat, 0)
    lax.fori_loop(1, LEVS, greet_lev, 0)

    for t in range(ROWS):
        lon[pl.ds(t * NV, NV), :] = jnp.full((NV, 128), lon_ref[t], jnp.int32)
    row = iota((NT, 2 * WAVES), 0)
    col = iota((NT, 2 * WAVES), 1)
    pick = one_hot(row == ROUNDS * (8 * (col >> 4) + (col & 7)))
    waves = jnp.broadcast_to(wave_row_ref[...].reshape(1, NT).astype(F32), (8, NT)).astype(BF16)
    place = dot(waves, pick).astype(jnp.int32)
    target = WAVES * (place & 1) + 128 * ((iota((8, 2 * WAVES), 1) >> 3) & 1) + (place >> 1)
    route[...] = one_hot(iota((2 * WAVES, 2 * WAVES), 0) == target[:1])
    row = iota((NV * PAD, ROWS * NV), 0)
    col = iota((NV * PAD, ROWS * NV), 1)
    at = lax.rem(row, PAD)
    at = jnp.where(me < LATS // 2, at, ROWS - 1 - at)
    order[...] = one_hot((lax.div(col, NV) == at) & (lax.rem(col, NV) == lax.div(row, PAD)))
    latitude = me * ROWS + lax.div(iota((ROWS * NV, 128), 0), NV)
    latitude = jnp.minimum(latitude, NT - 1 - latitude)
    over = jnp.where(lon[...] > 512 * (((latitude + EDGE) >> 7) + 1), 1.0, 0.0)
    over = jnp.broadcast_to(jnp.max(over, axis=0, keepdims=True), (PAD - ROWS, 128))
    flag_ref[...] = over
    folded[...] = jnp.zeros_like(folded)
    edges[...] = jnp.zeros_like(edges)

    lane_block = lax.div(iota((PAD, 128), 1), 16)

    def fourier(r):
        odd = lax.rem(r, 2)
        first = dot(x[:, :, : NLON // 2].reshape(ROWS * NV, NLON // 2), basis[r])
        second = dot(x[:, :, NLON // 2 :].reshape(ROWS * NV, NLON // 2), basis[r])
        values = first + second * jnp.where((iota((1, 2 * WAVES), 1) >> 8) == odd, 1.0, -1.0)
        column = iota((8, 2 * WAVES), 1)
        column = 2 * (column & 127) + (column >> 8)
        waves = r * WAVES + jnp.where(odd == 1, WAVES - 1 - column, column)
        twice = jnp.broadcast_to(2 * waves[:1], (ROWS * NV, 2 * WAVES))
        longitudes = jnp.concatenate([lon[...]] * 4, axis=1)
        values = jnp.where(twice < longitudes, values, 0.0).astype(BF16)
        values = dot(order[...], values).astype(BF16)
        values = dot(values, route[...])
        for high in range(LATS // 8):
            blocks = []
            for v in range(NV):
                block = values[v * PAD : (v + 1) * PAD, high * 128 : (high + 1) * 128]
                blocks.append(pltpu.roll(block, 16 * v, 1) if v else block)
            for bit in range(3):
                taken = (lane_block >> bit) & 1 == 1
                blocks = [jnp.where(taken, blocks[(i + (1 << bit)) % 8], blocks[i]) for i in range(8)]
            for low in range(8):
                block = jnp.concatenate([blocks[-low % 8][:ROWS], over], axis=0)
                sent[r, high * 8 + low] = block.astype(BF16)

    def send_lat(r):
        group = jnp.where((r == 0) & (pair < POLAR), ROUNDS, r) if plan.sparse else r

        for k in PEERS:
            peer = me ^ k
            pltpu.make_async_remote_copy(
                src_ref=sent.at[r, peer],
                dst_ref=got.at[r, me],
                send_sem=lat_send.at[r],
                recv_sem=lat_recv.at[group],
                device_id=(peer, lev),
                device_id_type=MESH,
            ).start()

    def send_lev(source, place, send, recv):
        for k in (4, 3, 5, 2, 6, 1, 7):
            peer = (lev + k) & (LEVS - 1)
            pltpu.make_async_remote_copy(
                src_ref=source.at[peer],
                dst_ref=place.at[lev],
                send_sem=send,
                recv_sem=recv,
                device_id=(me, peer),
                device_id_type=MESH,
            ).start()

    def edge_place(r, part):
        return (1, part) if r == 4 else (0, 2 * (r - 1) + part)

    def turn(chunk):
        r, low, high = plan.chunks[chunk]
        first, last = plan.sources(chunk)
        group = ROUNDS if plan.sparse and chunk == 0 else r
        mine = (pair >= first) & (pair < last)
        messages = 2 * (last - first)

        @pl.when(mine)
        def _():
            await_bytes(got.at[r, pl.ds(0, messages - 1)], lat_recv.at[group])
            got[r, me] = sent[r, me]

        if messages < LATS:

            @pl.when(jnp.logical_not(mine))
            def _():
                await_bytes(got.at[r, pl.ds(0, messages)], lat_recv.at[group])

        for i in plan.pairs(chunk):
            north = got[r, i].astype(F32)
            south = got[r, LATS - 1 - i].astype(F32)
            folded[0, pl.ds(i * ROWS, ROWS), :] = north[:ROWS] + south[:ROWS]
            folded[1, pl.ds(i * ROWS, ROWS), :] = north[:ROWS] - south[:ROWS]
            if r == 0:
                flag_ref[...] = jnp.maximum(flag_ref[...], jnp.maximum(north[ROWS:], south[ROWS:]))
        row = iota((128, 128), 0)
        col = iota((128, 128), 1)
        source = 16 * (((row & 7) + me) & 7) + 8 * ((row >> 3) & 1) + (row >> 4)
        pick = one_hot(col == source)
        for part in range(2):
            values = dot_nt(pick, folded[part, low:high].astype(BF16)).astype(BF16)
            turned[chunk][:, part] = values.reshape(LEVS, 16, high - low)
        send_lev(turned[chunk], ready[chunk], lev_send.at[chunk], lev_recv.at[chunk])
        if plan.sparse and r:
            for part in range(2):
                values = dot_nt(pick, folded[part, low - 128 : low].astype(BF16))
                tile, block = edge_place(r, part)
                values = pltpu.roll(values, (EDGE * block + EDGE) % 128, 1)
                edges[tile] = jnp.where((col >> 4) == block, values, edges[tile])
            if r in (1, 4):
                edge_sent[tile] = edges[tile].astype(BF16).reshape(LEVS, 16, 128)
                send_lev(edge_sent.at[tile], edge_got.at[tile], edge_send.at[tile], edge_recv.at[tile])

    def vertical_operator():
        pick_out = one_hot(iota((128, 64), 1) == (iota((128, 64), 0) >> 1))
        col = iota((64, 128), 1)
        pick_in = one_hot(iota((64, 128), 0) == 8 * (col >> 4) + (col & 7))
        same = (iota((128, 128), 0) & 1) == ((iota((128, 128), 1) >> 3) & 1)
        whole = vertical_ref[...]
        high = whole.astype(BF16)
        low = (whole - high.astype(F32)).astype(BF16)
        for k, term in enumerate((high, low)):
            term = dot_nt(pick_out, term).astype(BF16)
            term = dot(term, pick_in)
            mix[:, pl.ds(128 * k, 128)] = jnp.where(same, term, 0.0).astype(BF16)

    def mixed(values):
        values = values.reshape(128, values.shape[-1])
        return dot(mix[...], jnp.concatenate([values, values], axis=0))

    def received(chunk, part):
        if part == 0:
            await_bytes(ready[chunk].at[pl.ds(0, LEVS - 1)], lev_recv.at[chunk])
            ready[chunk][lev] = turned[chunk][lev]
        return mixed(ready[chunk][:, part]).astype(BF16)

    edge_values = {}

    def edge_piece(r, part):
        tile, block = edge_place(r, part)
        if tile not in edge_values:
            await_bytes(edge_got.at[tile, pl.ds(0, LEVS - 1)], edge_recv.at[tile])
            edge_got[tile, lev] = edge_sent[tile, lev]
            edge_values[tile] = mixed(edge_got[tile])
        piece = pltpu.roll(edge_values[tile], (128 - EDGE - EDGE * block) % 128, 1)
        return jnp.where(iota((128, 128), 1) >= 128 - EDGE, piece, 0.0).astype(BF16)

    def legendre(r):
        width = HALF - 128 * r
        wave = wave_ref[(me * LEVS + lev) * ROUNDS + r]
        for part in range(2):
            pieces = [received(k, part) for k in range(count) if plan.chunks[k][0] == r]
            if plan.sparse and r:
                pieces.insert(0, edge_piece(r, part))
            values = jnp.concatenate(pieces, axis=1) if len(pieces) > 1 else pieces[0]
            table_copies[r, part].wait()
            start = plan.table_start(r)
            total = dot(values, table[r, start:, pl.ds(part * HALF, width)])
            degree = wave + 2 * iota((128, width), 1) + part
            total = jnp.where(degree < NT, total, 0.0)
            result[r, :, :, pl.ds(part * HALF, width)] = total.reshape(64, 2, width)
            if width < HALF:
                result[r, :, :, pl.ds(part * HALF + width, HALF - width)] = jnp.zeros((64, 2, HALF - width), F32)
        pltpu.make_async_copy(result.at[r], out_ref.at[:, r], out_sem.at[r]).start()

    grid_copy.wait()

    def advance(step, carry):
        r, due = round_at(step)

        @pl.when(due)
        def _():
            basis_copy(r).wait()
            fourier(r)

        @pl.when(step == 0)
        def _():
            pl.semaphore_wait(barrier, LATS - 1 + LEVS - 1)

        @pl.when(due)
        def _():
            send_lat(r)

        @pl.when(step == 0)
        def _():
            vertical_operator()

        for chunk in range(count):

            @pl.when(step == plan.turn_step[chunk])
            def _():
                turn(chunk)

        return carry

    lax.fori_loop(0, max(plan.turn_step) + 1, advance, 0)
    flag_out[0] = (jnp.max(flag_ref[...]) > 0).astype(jnp.int32)
    for r in plan.sums:
        legendre(r)
    for r in range(ROUNDS):
        pltpu.make_async_copy(result.at[r], out_ref.at[:, r], out_sem.at[r]).wait()

    def drain_lat(r, carry):
        @pl.when(sends(r))
        def _():
            await_bytes(sent.at[r, pl.ds(0, LATS - 1)], lat_send.at[r])

        return carry

    lax.fori_loop(0, ROUNDS, drain_lat, 0)
    for chunk in range(count):
        await_bytes(turned[chunk].at[pl.ds(0, LEVS - 1)], lev_send.at[chunk])
    if plan.sparse:
        for tile in range(2):
            await_bytes(edge_sent.at[tile, pl.ds(0, LEVS - 1)], edge_send.at[tile])


def transform(plan, collective_id, wave_table, wave_row, lon_count, vertical, grid_field, basis, legendre):
    anywhere = pl.BlockSpec(memory_space=pl.ANY)
    vmem = pl.BlockSpec(memory_space=pltpu.VMEM)
    smem = pl.BlockSpec(memory_space=pltpu.SMEM)
    count = len(plan.chunks)
    chunk_shapes = [pltpu.VMEM((LEVS, 2, 16, high - low), BF16) for _, low, high in plan.chunks]
    return pl.pallas_call(
        functools.partial(kernel, plan),
        out_shape=[
            jax.ShapeDtypeStruct((64, ROUNDS, 2, NT), F32),
            jax.ShapeDtypeStruct((1,), jnp.int32),
        ],
        in_specs=[smem, smem, vmem, vmem, anywhere, anywhere, anywhere],
        out_specs=[anywhere, smem],
        scratch_shapes=[
            pltpu.VMEM((ROWS, NV, NLON), BF16),
            pltpu.VMEM((PAD - ROWS, 128), F32),
            pltpu.VMEM((ROUNDS, NLON // 2, 2 * WAVES), BF16),
            pltpu.VMEM((ROUNDS, HALF, NT), BF16),
            pltpu.VMEM((ROWS * NV, 128), jnp.int32),
            pltpu.VMEM((2 * WAVES, 2 * WAVES), BF16),
            pltpu.VMEM((NV * PAD, ROWS * NV), BF16),
            pltpu.VMEM((128, 256), BF16),
            pltpu.VMEM((2, HALF, 128), F32),
            pltpu.VMEM((2, 128, 128), F32),
            pltpu.VMEM((ROUNDS, LATS, PAD, 128), BF16),
            pltpu.VMEM((ROUNDS, LATS, PAD, 128), BF16),
            pltpu.VMEM((2, LEVS, 16, 128), BF16),
            pltpu.VMEM((2, LEVS, 16, 128), BF16),
            pltpu.VMEM((ROUNDS, 64, 2, NT), F32),
            *chunk_shapes,
            *chunk_shapes,
            pltpu.SemaphoreType.DMA,
            pltpu.SemaphoreType.DMA((ROUNDS,)),
            pltpu.SemaphoreType.DMA((ROUNDS, 2)),
            pltpu.SemaphoreType.DMA((ROUNDS,)),
            pltpu.SemaphoreType.DMA((ROUNDS,)),
            pltpu.SemaphoreType.DMA((ROUNDS + 1,)),
            pltpu.SemaphoreType.DMA((count,)),
            pltpu.SemaphoreType.DMA((count,)),
            pltpu.SemaphoreType.DMA((2,)),
            pltpu.SemaphoreType.DMA((2,)),
        ],
        compiler_params=pltpu.CompilerParams(
            collective_id=collective_id, has_side_effects=True, vmem_limit_bytes=56 << 20
        ),
        cost_estimate=pl.CostEstimate(flops=6_000_000_000, bytes_accessed=24_000_000, transcendentals=0),
    )(wave_table, lon_count, wave_row, vertical, grid_field, basis, legendre)


def on_device(grid_field, lon_count, wave_table, legendre, vertical):
    basis = jnp.asarray(basis_constant())
    args = (wave_table, wave_table, lon_count, vertical, grid_field, basis, legendre)
    spectral, flag = transform(Plan(True), 0, *args)
    spectral = lax.cond(
        flag[0] > 0, lambda kept, *rest: transform(Plan(False), 1, *rest)[0], lambda kept, *rest: kept, spectral, *args
    )
    return spectral.transpose(0, 2, 1, 3)


def solution(mesh):
    return jax.shard_map(
        on_device,
        mesh=mesh,
        in_specs=(P("lat", "lev", None), P("lat"), P(), P(("lat", "lev"), None, None), P()),
        out_specs=P(None, None, ("lat", "lev"), None),
        check_vma=False,
    )
```
